32 devices in a mesh: groups: 2 (over y), dom: 4 (over z), orient: 2 (over x), shell: 2 (over core).
Axes of the slice: x: 2, y: 2, z: 4, core: 2. Of those that a mesh axis runs over, the one named last changes fastest.
Arguments:
- tiles: bfloat16 [64, 128, 128], P(('groups', 'dom')), parts along dimension 0, may hold values from -6 to 6
- particle_tile: int32 [512], P('groups'), parts along dimension 0, may hold values from 0 to 31, as said below
- particle_offset: int32 [512, 2], P('groups'), parts along dimension 0, may hold values from 0 to 32
- wedge_slope: int32 [32], P('groups'), parts along dimension 0, may hold values from 60 to 240
- rot_ref: bfloat16 [384, 18432], P(('groups', 'orient'), ('dom', 'shell')), parts along dimension 0, may hold values from -160 to 160
Outputs:
- new_reference: float32 [384, 18432], P(('groups', 'orient'), ('dom', 'shell')), parts along dimension 0
- particle_logz: float32 [512], P(('groups', 'dom')), parts along dimension 0
The draws below stay inside these ranges and needn't reach their ends.
There are 2 independent parts, one for each index of `groups`. The reference program is written for one: setup_inputs(seed, part) draws one part's arguments, and reference() takes and returns one part's arrays. A program takes and returns all parts, laid end to end along the dimension named above; each array names one. Nothing has to cross between parts.
Inputs may be any that keep to these rules, and one draw needn't show every extreme that they name: `particle_tile`: each aligned block of 64 particles holds at most 32 particles whose tiles lie in one range k * 8 to (k + 1) * 8 - 1, and exactly 32 for some such range in every block.
All inputs are finite; a program needn't handle non-finite values.
Results may differ from the reference program's by a relative error of at most 0.0015.
The reference program's roundings to bfloat16 on the way (of `boxes`, `spectra`, `weighted` and `weights`) count: a program that leaves them out, or rounds other values in their place, can miss the bound.
Values may be sent and summed in bfloat16 or wider, within the bound.
A program may use at most 64 MiB of HBM per device.

```python
import math
import jax
import jax.numpy as jnp
from jax import lax

BOX = 96
TILE = 128
TILE_DEV = 8
PART_DEV = 64
TOMOS = 16
TILES = 32
PARTICLES = 256
ORIENTS = 192
KTOT = 18432


def draw_particle_tile(key, part):
    owners = PARTICLES // PART_DEV
    slot_count = 2 * PART_DEV // owners

    def one_block(block_key):
        pick_key, rank_key, tile_key, order_key = jax.random.split(block_key, 4)
        busiest = jax.random.randint(pick_key, (), 0, owners)
        source = jnp.arange(owners * slot_count, dtype=jnp.int32) // slot_count
        ranking = jax.random.permutation(rank_key, owners * slot_count).astype(jnp.int32)
        ranking = jnp.where(source == busiest, -1, ranking)
        chosen = jnp.argsort(ranking, stable=True)[:PART_DEV]
        chosen = chosen[jax.random.permutation(order_key, PART_DEV)]
        local_tile = jax.random.randint(tile_key, (PART_DEV,), 0, TILE_DEV)
        return (source[chosen] * TILE_DEV + local_tile).astype(jnp.int32)
    return jax.vmap(one_block)(jax.random.split(key, owners)).reshape(PARTICLES)


def draw_rot_ref(key, part):
    base_key = jax.random.fold_in(key, 0)
    values = jax.random.truncated_normal(base_key, -4.0, 4.0, (ORIENTS, KTOT), jnp.float32)
    return values.astype(jnp.bfloat16)


def set_ends(drawn, own_key, smallest, largest):
    place = [jax.random.randint(jax.random.fold_in(own_key, axis), (), 0, length) for axis, length in enumerate(drawn.shape)]
    widest = drawn.shape.index(max(drawn.shape))
    next_to = place[:widest] + [(place[widest] + 1) % drawn.shape[widest]] + place[widest + 1:]
    return drawn.at[tuple(place)].set(smallest).at[tuple(next_to)].set(largest)


def steps_of(rng, extent, cuts, low, high):
    loudness, own = 1.0, jax.random.fold_in(rng, 6)
    for dim, shards_of in cuts:
        heights = jnp.exp(jax.random.uniform(jax.random.fold_in(own, dim), (shards_of,), jnp.float32, low / len(cuts), high / len(cuts)))
        loudness = loudness * jnp.repeat(heights, extent[dim] // shards_of).reshape([-1 if axis == dim else 1 for axis in range(len(extent))])
    return loudness


def centred(key, extent, scale, most, shards=(), kind=jnp.bfloat16):
    array = scale * jax.random.normal(key, extent, jnp.float32)
    if shards:
        array = array * steps_of(key, extent, shards, -0.22, 0.18)
    return jnp.clip(array, -most, most).astype(kind)


def setup_inputs(seed: int = 0, part: int = 0) -> dict:
    splits = jax.random.split(jax.random.key(seed), 6)
    part_splits = jax.random.split(jax.random.fold_in(splits[5], part), 6)
    return {
        "tiles": centred(part_splits[0], (TILES, TILE, TILE), 1.0, 6.0, ((0, 4),)),
        "particle_tile": draw_particle_tile(jax.random.fold_in(jax.random.fold_in(splits[5], part), 71), part),
        "particle_offset": set_ends(jax.random.randint(part_splits[2], (PARTICLES, 2), 0, TILE - BOX + 1), jax.random.fold_in(part_splits[2], 1), 0, TILE - BOX).astype(jnp.int32),
        "wedge_slope": set_ends(jax.random.randint(part_splits[3], (TOMOS,), 60, 241), jax.random.fold_in(part_splits[3], 1), 60, 240).astype(jnp.int32),
        "rot_ref": draw_rot_ref(jax.random.fold_in(jax.random.fold_in(splits[5], part), 71), part),
    }


def box_tables(kx_rows, box_width):
    positions = jnp.arange(box_width, dtype=jnp.int32)
    angle_step = 2.0 * math.pi / box_width
    phase_x = ((kx_rows[:, None] * positions[None, :]) % box_width).astype(jnp.float32) * angle_step
    phase_y = ((positions[:, None] * positions[None, :]) % box_width).astype(jnp.float32) * angle_step
    return jnp.cos(phase_x), jnp.sin(phase_x), jnp.cos(phase_y), jnp.sin(phase_y)


def transform(boxes, tables, box_width):
    cos_x, sin_x, cos_y, sin_y = tables
    highest = lax.Precision.HIGHEST
    values = boxes.astype(jnp.float32)
    real_y = jnp.einsum("pyx,kx->pyk", values, cos_x, precision=highest)
    imag_y = -jnp.einsum("pyx,kx->pyk", values, sin_x, precision=highest)
    real_f = jnp.einsum("qy,pyk->pkq", cos_y, real_y, precision=highest) + jnp.einsum("qy,pyk->pkq", sin_y, imag_y, precision=highest)
    imag_f = jnp.einsum("qy,pyk->pkq", cos_y, imag_y, precision=highest) - jnp.einsum("qy,pyk->pkq", sin_y, real_y, precision=highest)
    spectrum = jnp.stack([real_f, imag_f], axis=2) * (1.0 / box_width)
    return spectrum.reshape(boxes.shape[0], -1).astype(jnp.bfloat16)


def wedge_grid(wedge_slope, kx_rows, box_width):
    freq_y = jnp.arange(box_width, dtype=jnp.int32)
    along_y = jnp.minimum(freq_y, box_width - freq_y)
    along_x = jnp.minimum(kx_rows, box_width - kx_rows)
    inside = along_y[None, None, :] * 100 <= wedge_slope[:, None, None] * along_x[None, :, None]
    grid = jnp.broadcast_to(inside[:, :, None, :], (wedge_slope.shape[0], kx_rows.shape[0], 2, box_width))
    return grid.reshape(wedge_slope.shape[0], -1).astype(jnp.float32)


def reference(tiles, particle_tile, particle_offset, wedge_slope, rot_ref):
    def cut_box(tile_row, offset_y, offset_x):
        return lax.dynamic_slice(tiles, (tile_row, offset_y, offset_x), (1, BOX, BOX))[0]

    boxes = jax.vmap(cut_box)(particle_tile, particle_offset[:, 0], particle_offset[:, 1])
    all_rows = jnp.arange(BOX, dtype=jnp.int32)
    tables = box_tables(all_rows, BOX)
    wedge = wedge_grid(wedge_slope, all_rows, BOX)
    tomograms = particle_tile % TOMOS
    block_size = 64

    def weigh(inputs):
        group_boxes, group_tomo = inputs
        spectra = transform(group_boxes, tables, BOX)
        return spectra * wedge[group_tomo].astype(jnp.bfloat16)

    weighted = lax.map(weigh, (boxes.reshape(-1, block_size, BOX, BOX), tomograms.reshape(-1, block_size)))
    weighted = weighted.reshape(PARTICLES, KTOT)
    scores = jnp.dot(weighted, rot_ref.T, preferred_element_type=jnp.float32) * (6.0 / BOX)
    row_top = jnp.max(scores, axis=1)
    shifted = jnp.exp(scores - row_top[:, None])
    row_total = jnp.sum(shifted, axis=1)
    particle_logz = row_top + jnp.log(row_total)
    weights = (shifted / row_total[:, None]).astype(jnp.bfloat16)
    numerator = jnp.dot(weights.T, weighted, preferred_element_type=jnp.float32)
    tomo_hot = (tomograms[:, None] == jnp.arange(TOMOS, dtype=jnp.int32)[None, :]).astype(jnp.bfloat16)
    tomo_weight = jnp.dot(tomo_hot.T, weights, preferred_element_type=jnp.float32)
    denominator = jnp.dot(tomo_weight.T, wedge, precision=lax.Precision.HIGHEST, preferred_element_type=jnp.float32)
    return numerator / (denominator + 1.0), particle_logz
```

```python
import functools
import math

import jax
import jax.numpy as jnp
import numpy as np
from jax import lax
from jax.experimental import pallas as pl
from jax.experimental.pallas import tpu as pltpu
from jax.sharding import PartitionSpec as P

BOX = 96
TOMOS = 16
LANES = 128
MESH = pl.DeviceIdType.MESH
VMEM = pl.BlockSpec(memory_space=pltpu.VMEM)
SMEM = pl.BlockSpec(memory_space=pltpu.SMEM)
ANY = pl.BlockSpec(memory_space=pl.ANY)
F32 = jnp.float32
BF16 = jnp.bfloat16
LIMIT = 56 * 1024 * 1024


def round_up(value, step):
    return -(-value // step) * step


def place(name, axis):
    return {name: axis}


def greet(peers):
    barrier = pltpu.get_barrier_semaphore()
    for peer in peers:
        pl.semaphore_signal(barrier, inc=1, device_id=peer, device_id_type=MESH)
    pl.semaphore_wait(barrier, len(peers))


def gather_kernel(
    doms, orients, shells, mine_ref, all_ref, own_sem, z_send, z_recv, x_send, x_recv, c_send, c_recv
):
    dom = lax.axis_index("dom")
    orient = lax.axis_index("orient")
    shell = lax.axis_index("shell")
    rows = mine_ref.shape[0]
    piece = rows // (orients * shells)
    z_peers = [lax.rem(dom + r, doms) for r in range(1, doms)]
    x_peers = [lax.rem(orient + r, orients) for r in range(1, orients)]
    c_peers = [lax.rem(shell + r, shells) for r in range(1, shells)]
    greet(
        [{"dom": z} for z in z_peers]
        + [{"orient": x} for x in x_peers]
        + [{"shell": c} for c in c_peers]
    )

    def part(block, x, c):
        start = pl.multiple_of(block * rows + (x * shells + c) * piece, 16)
        return all_ref.at[pl.ds(start, piece)]

    own = pltpu.make_async_copy(
        mine_ref, all_ref.at[pl.ds(pl.multiple_of(dom * rows, 16), rows)], own_sem
    )
    own.start()
    first = pl.multiple_of((orient * shells + shell) * piece, 16)
    started = []

    def send(source, target, send_sem, recv_sem, device):
        copy = pltpu.make_async_remote_copy(
            src_ref=source,
            dst_ref=target,
            send_sem=send_sem,
            recv_sem=recv_sem,
            device_id=device,
            device_id_type=MESH,
        )
        copy.start()
        started.append(copy)

    def arrived(target, send_sem, recv_sem, device):
        pltpu.make_async_remote_copy(
            src_ref=target,
            dst_ref=target,
            send_sem=send_sem,
            recv_sem=recv_sem,
            device_id=device,
            device_id_type=MESH,
        ).wait_recv()

    for r, z in enumerate(z_peers):
        send(
            mine_ref.at[pl.ds(first, piece)],
            part(dom, orient, shell),
            z_send.at[r],
            z_recv.at[dom],
            {"dom": z},
        )
    for r, z in enumerate(z_peers):
        held = part(z, orient, shell)
        arrived(held, z_send.at[r], z_recv.at[z], {"dom": z})
        for i, x in enumerate(x_peers):
            send(held, held, x_send.at[r, i], x_recv.at[z, orient], {"orient": x})
        for i, c in enumerate(c_peers):
            send(held, held, c_send.at[r, 0, i], c_recv.at[z, orient, shell], {"shell": c})
    for r, z in enumerate(z_peers):
        for k, x in enumerate(x_peers):
            held = part(z, x, shell)
            arrived(held, x_send.at[r, k], x_recv.at[z, x], {"orient": x})
            for i, c in enumerate(c_peers):
                send(held, held, c_send.at[r, 1 + k, i], c_recv.at[z, x, shell], {"shell": c})
    for r, z in enumerate(z_peers):
        for k in range(orients):
            x = lax.rem(orient + k, orients)
            for i, c in enumerate(c_peers):
                arrived(part(z, x, c), c_send.at[r, k, i], c_recv.at[z, x, c], {"shell": c})
    own.wait()
    for copy in started:
        copy.wait_send()


def gather_tiles(mine, doms, orients, shells):
    dma = pltpu.SemaphoreType.DMA
    return pl.pallas_call(
        functools.partial(gather_kernel, doms, orients, shells),
        out_shape=jax.ShapeDtypeStruct((doms * mine.shape[0], mine.shape[1]), mine.dtype),
        in_specs=[ANY],
        out_specs=ANY,
        scratch_shapes=[
            dma,
            dma((doms,)),
            dma((doms,)),
            dma((doms, orients)),
            dma((doms, orients)),
            dma((doms, orients, shells)),
            dma((doms, orients, shells)),
        ],
        compiler_params=pltpu.CompilerParams(collective_id=0, has_side_effects=True),
        name="gather_tiles",
    )(mine)


def split(values):
    high = values.astype(BF16)
    return high, (values - high.astype(F32)).astype(BF16)


def grid_rows(kx_first, width):
    lane = lax.broadcasted_iota(jnp.int32, (1, width), 1)
    kx_step = jnp.zeros_like(lane)
    ky = lane
    for edge in range(BOX, width, BOX):
        over = (lane >= edge).astype(jnp.int32)
        ky = ky - BOX * over
        if edge % (2 * BOX) == 0:
            kx_step = kx_step + over
    kx = kx_first + kx_step
    along_y = jnp.minimum(ky, BOX - ky) * 100
    along_x = jnp.minimum(kx, BOX - kx)
    return along_y.astype(F32), along_x.astype(F32)


def spectra_kernel(
    sub_rows,
    shells,
    code_ref,
    slope_ref,
    tiles_ref,
    x_ref,
    y_ref,
    rot_ref,
    weighted_ref,
    scores_ref,
    hot_ref,
    tile_t,
    x_tab,
    held,
    slopes,
    tomos,
):
    position = lax.axis_index("dom") * shells + lax.axis_index("shell")
    rows = x_ref.shape[1]
    particles = slopes.shape[0]
    base = x_ref[position]
    for shift in range(x_tab.shape[0]):
        moved = base if shift == 0 else pltpu.roll(base, shift, 1)
        high = moved.astype(BF16).astype(F32)
        x_tab[shift] = jnp.concatenate([high, moved - high], axis=0).astype(BF16)

    @pl.loop(0, tiles_ref.shape[0])
    def _(tile):
        tile_t[tile] = tiles_ref[tile].astype(F32).T.astype(BF16)

    unroll = 8

    @pl.loop(0, particles // unroll)
    def _(step):
        for part in range(unroll):
            particle = step * unroll + part
            code = code_ref[particle]
            tile = code >> 12
            start_y = (code >> 6) & 63
            start_x = code & 63
            both = jnp.dot(x_tab[start_x], tile_t[tile], preferred_element_type=F32)
            along = both[:rows] + both[rows:]
            along = pltpu.roll(along, (LANES - start_y) & (LANES - 1), 1)
            held[pl.ds(pl.multiple_of(particle * rows, 8), rows), :] = along
            tomo = lax.rem(tile, TOMOS)
            slope = slope_ref[tomo].astype(F32)
            slopes[pl.ds(particle, 1), :] = jnp.full((1, LANES), slope, F32)
            tomos[pl.ds(particle, 1), :] = jnp.full((1, LANES), tomo, jnp.int32)

    lane = lax.broadcasted_iota(jnp.int32, tomos.shape, 1)
    hot_ref[...] = jnp.where(tomos[...] == lane, 1.0, 0.0).astype(BF16)
    kx_first = position * sub_rows
    chunk = 256

    @pl.loop(0, particles // chunk)
    def _(block):
        first = pl.multiple_of(block * chunk, chunk)
        own_slope = slopes[pl.ds(first, chunk), :][:, :1]

        def lines(row, side):
            real = held[pl.ds(first * rows + row, chunk, stride=rows), :]
            imag = held[pl.ds(first * rows + sub_rows + row, chunk, stride=rows), :]
            high, low = split(jnp.concatenate([real, imag], axis=1))
            return (
                jnp.dot(high, y_ref[side, 0], preferred_element_type=F32)
                + jnp.dot(high, y_ref[side, 1], preferred_element_type=F32)
                + jnp.dot(low, y_ref[side, 0], preferred_element_type=F32)
            )

        for row in range(0, sub_rows, 2):
            even = lines(row, 0)
            if row + 1 < sub_rows:
                odd = lines(row + 1, 1)
                values = jnp.concatenate(
                    [even[:, :LANES], even[:, LANES:] + odd[:, :LANES], odd[:, LANES:]], axis=1
                )
            else:
                values = even[:, : 2 * BOX]
            width = values.shape[1]
            along_y, along_x = grid_rows(kx_first + row, width)
            inside = along_y <= own_slope * along_x
            values = jnp.where(inside, values * (1.0 / BOX), 0.0)
            weighted_ref[pl.ds(first, chunk), row * 2 * BOX : row * 2 * BOX + width] = values.astype(
                BF16
            )
        scores = lax.dot_general(
            weighted_ref[pl.ds(first, chunk), :],
            rot_ref[...],
            (((1,), (1,)), ((), ())),
            preferred_element_type=F32,
        )
        pad = scores_ref.shape[1] - scores.shape[1]
        scores_ref[pl.ds(first, chunk), :] = jnp.concatenate(
            [scores, jnp.zeros((chunk, pad), F32)], axis=1
        )


def spectra_and_scores(code, wedge_slope, tiles, rot_ref, doms, shells):
    sub_rows = BOX // (doms * shells)
    rows = round_up(2 * sub_rows, 8)
    shifts = tiles.shape[1] - BOX + 1
    angle = 2.0 * math.pi / BOX
    kx = np.arange(BOX)
    phase = angle * ((kx[:, None] * kx[None, :]) % BOX)
    x_table = np.zeros((doms * shells, rows, LANES), np.float32)
    for position in range(doms * shells):
        own = slice(position * sub_rows, (position + 1) * sub_rows)
        x_table[position, :sub_rows, :BOX] = np.cos(phase[own])
        x_table[position, sub_rows : 2 * sub_rows, :BOX] = -np.sin(phase[own])
    y_real = np.zeros((2 * LANES, 2 * BOX), np.float32)
    y_real[:BOX, :BOX] = np.cos(phase)
    y_real[:BOX, BOX:] = -np.sin(phase)
    y_real[LANES : LANES + BOX, :BOX] = np.sin(phase)
    y_real[LANES : LANES + BOX, BOX:] = np.cos(phase)
    gap = 2 * LANES - 2 * BOX
    sides = np.stack([np.pad(y_real, ((0, 0), (0, gap))), np.pad(y_real, ((0, 0), (gap, 0)))])
    high = sides.astype(BF16)
    low = (sides - high.astype(np.float32)).astype(BF16)
    y_table = np.stack([high, low], axis=1)
    particles = code.shape[0]
    depth = rot_ref.shape[1]
    width = round_up(rot_ref.shape[0] + 1, LANES)
    return pl.pallas_call(
        functools.partial(spectra_kernel, sub_rows, shells),
        out_shape=(
            jax.ShapeDtypeStruct((particles, depth), BF16),
            jax.ShapeDtypeStruct((particles, width), F32),
            jax.ShapeDtypeStruct((particles, LANES), BF16),
        ),
        in_specs=[SMEM, SMEM, VMEM, VMEM, VMEM, VMEM],
        out_specs=(VMEM, VMEM, VMEM),
        scratch_shapes=[
            pltpu.VMEM(tiles.shape, BF16),
            pltpu.VMEM((shifts, 2 * rows, LANES), BF16),
            pltpu.VMEM((particles * rows, LANES), F32),
            pltpu.VMEM((particles, LANES), F32),
            pltpu.VMEM((particles, LANES), jnp.int32),
        ],
        compiler_params=pltpu.CompilerParams(vmem_limit_bytes=LIMIT),
        name="spectra_and_scores",
    )(code, wedge_slope, tiles, x_table, y_table, rot_ref)


def softmax_kernel(
    doms, orients, shells, owned, partial_ref, weights_ref, scores, outgoing, s_send, s_recv, w_send, w_recv
):
    count = doms * orients * shells
    dom = lax.axis_index("dom")
    orient = lax.axis_index("orient")
    shell = lax.axis_index("shell")
    me = (dom * orients + orient) * shells + shell
    barrier = pltpu.get_barrier_semaphore()

    def device(index):
        return {
            "dom": index // (orients * shells),
            "orient": (index // shells) % orients,
            "shell": index % shells,
        }

    def each(body):
        @pl.loop(1, count)
        def _(step):
            body(lax.rem(me + step, count))

    def remote(source, target, send_sem, recv_sem, index):
        return pltpu.make_async_remote_copy(
            src_ref=source,
            dst_ref=target,
            send_sem=send_sem,
            recv_sem=recv_sem,
            device_id=device(index),
            device_id_type=MESH,
        )

    each(lambda j: pl.semaphore_signal(barrier, inc=1, device_id=device(j), device_id_type=MESH))
    pl.semaphore_wait(barrier, count - 1)
    each(
        lambda j: remote(
            partial_ref.at[j], scores.at[me], s_send.at[j], s_recv.at[me], j
        ).start()
    )
    scores[me] = partial_ref[me]
    each(
        lambda j: remote(
            partial_ref.at[j], scores.at[j], s_send.at[j], s_recv.at[j], j
        ).wait_recv()
    )
    rows, width = scores.shape[1:]
    lane = lax.broadcasted_iota(jnp.int32, (rows, width), 1)
    real = lane < owned
    halves = []
    for half in range(orients):
        total = jnp.zeros((rows, width), F32)
        for block in range(doms):
            for side in range(shells):
                total = total + scores[(block * orients + half) * shells + side]
        halves.append(jnp.where(real, total * (6.0 / BOX), -3e38))
    top = halves[0]
    for half in halves[1:]:
        top = jnp.maximum(top, half)
    row_top = jnp.max(top, axis=1, keepdims=True)
    shifted = [jnp.where(real, jnp.exp(half - row_top), 0.0) for half in halves]
    row_sum = shifted[0]
    for half in shifted[1:]:
        row_sum = row_sum + half
    row_total = jnp.sum(row_sum, axis=1, keepdims=True)
    logz = row_top + jnp.log(row_total)
    for half in range(orients):
        rounded = (shifted[half] / row_total).astype(BF16).astype(F32)
        outgoing[half] = jnp.where(lane == owned, logz, rounded)
    each(
        lambda j: remote(
            outgoing.at[(j // shells) % orients], weights_ref.at[me], w_send.at[j], w_recv.at[me], j
        ).start()
    )
    weights_ref[me] = outgoing[orient]
    each(
        lambda j: remote(
            outgoing.at[(j // shells) % orients], weights_ref.at[j], w_send.at[j], w_recv.at[j], j
        ).wait_recv()
    )

    def finish(j):
        remote(partial_ref.at[j], scores.at[j], s_send.at[j], s_recv.at[j], j).wait_send()
        remote(
            outgoing.at[(j // shells) % orients], weights_ref.at[j], w_send.at[j], w_recv.at[j], j
        ).wait_send()

    each(finish)


def exchange_softmax(partial_scores, owned, doms, orients, shells):
    count = doms * orients * shells
    particles, width = partial_scores.shape
    blocks = partial_scores.reshape(count, particles // count, width)
    dma = pltpu.SemaphoreType.DMA
    weights = pl.pallas_call(
        functools.partial(softmax_kernel, doms, orients, shells, owned),
        out_shape=jax.ShapeDtypeStruct(blocks.shape, F32),
        in_specs=[VMEM],
        out_specs=VMEM,
        scratch_shapes=[
            pltpu.VMEM(blocks.shape, F32),
            pltpu.VMEM((orients,) + blocks.shape[1:], F32),
            dma((count,)),
            dma((count,)),
            dma((count,)),
            dma((count,)),
        ],
        compiler_params=pltpu.CompilerParams(collective_id=1, has_side_effects=True),
        name="exchange_softmax",
    )(blocks)
    return weights.reshape(particles, width)


def average_kernel(
    sub_rows, shells, owned, slope_ref, weights_ref, weighted_ref, hot_ref, out_ref, logz_ref
):
    dom = lax.axis_index("dom")
    position = dom * shells + lax.axis_index("shell")
    turned = weights_ref[...].T
    part_dev = logz_ref.shape[1]
    particles = turned.shape[1]
    logz_row = jnp.broadcast_to(turned[owned : owned + 1], (8, particles))
    logz_ref[...] = pltpu.roll(logz_row, lax.rem(particles - dom * part_dev, particles), 1)[
        :1, :part_dev
    ]
    kept = turned[:owned].astype(BF16)
    tomo_weight = jnp.dot(kept, hot_ref[...], preferred_element_type=F32)[:, :TOMOS]
    pieces = []
    rest = tomo_weight
    for _ in range(3):
        piece = rest.astype(BF16)
        pieces.append(piece.astype(F32))
        rest = rest - pieces[-1]
    pieces = jnp.concatenate(pieces, axis=1).astype(BF16)
    tomo_row = lax.broadcasted_iota(jnp.int32, (TOMOS, 1), 0)
    slopes = jnp.zeros((TOMOS, 1), F32)
    for tomo in range(TOMOS):
        slopes = jnp.where(tomo_row == tomo, slope_ref[tomo].astype(F32), slopes)
    for row in range(0, sub_rows, 2):
        width = min(2, sub_rows - row) * 2 * BOX
        along_y, along_x = grid_rows(position * sub_rows + row, width)
        wedge = jnp.where(along_y <= slopes * along_x, 1.0, 0.0)
        wedge = jnp.concatenate([wedge, wedge, wedge], axis=0).astype(BF16)
        span = slice(row * 2 * BOX, row * 2 * BOX + width)
        numerator = jnp.dot(kept, weighted_ref[:, span], preferred_element_type=F32)
        denominator = jnp.dot(pieces, wedge, preferred_element_type=F32)
        out_ref[:, span] = numerator / (denominator + 1.0)


def average(wedge_slope, weights, weighted, hot, owned, doms, shells):
    part_dev = weights.shape[0] // doms
    return pl.pallas_call(
        functools.partial(average_kernel, BOX // (doms * shells), shells, owned),
        out_shape=(
            jax.ShapeDtypeStruct((owned, weighted.shape[1]), F32),
            jax.ShapeDtypeStruct((1, part_dev), F32),
        ),
        in_specs=[SMEM, VMEM, VMEM, VMEM],
        out_specs=(VMEM, VMEM),
        compiler_params=pltpu.CompilerParams(vmem_limit_bytes=LIMIT),
        name="average",
    )(wedge_slope, weights, weighted, hot)


def local(tiles, particle_tile, particle_offset, wedge_slope, rot_ref):
    doms = lax.axis_size("dom")
    orients = lax.axis_size("orient")
    shells = lax.axis_size("shell")
    tile_dev, side, _ = tiles.shape
    code = particle_tile * 4096 + particle_offset[:, 0] * 64 + particle_offset[:, 1]
    gathered = gather_tiles(tiles.reshape(tile_dev * side, side), doms, orients, shells)
    weighted, partial_scores, hot = spectra_and_scores(
        code, wedge_slope, gathered.reshape(doms * tile_dev, side, side), rot_ref, doms, shells
    )
    owned = rot_ref.shape[0]
    weights = exchange_softmax(partial_scores, owned, doms, orients, shells)
    new_reference, logz = average(wedge_slope, weights, weighted, hot, owned, doms, shells)
    return new_reference, logz.reshape(-1)


def solution(mesh):
    in_specs = (
        P(("groups", "dom"), None, None),
        P("groups"),
        P("groups", None),
        P("groups"),
        P(("groups", "orient"), ("dom", "shell")),
    )
    out_specs = (P(("groups", "orient"), ("dom", "shell")), P(("groups", "dom")))
    return jax.shard_map(local, mesh=mesh, in_specs=in_specs, out_specs=out_specs, check_vma=False)
```

```python
import functools
import math

import jax
import jax.numpy as jnp
import numpy as np
from jax import lax
from jax.experimental import pallas as pl
from jax.experimental.pallas import tpu as pltpu
from jax.sharding import PartitionSpec as P

BOX = 96
TOMOS = 16
LANES = 128
MESH = pl.DeviceIdType.MESH
VMEM = pl.BlockSpec(memory_space=pltpu.VMEM)
SMEM = pl.BlockSpec(memory_space=pltpu.SMEM)
F32 = jnp.float32
BF16 = jnp.bfloat16
LIMIT = 56 * 1024 * 1024


def round_up(value, step):
    return -(-value // step) * step


def split(values):
    pieces = []
    for _ in range(3):
        pieces.append(values.astype(BF16))
        values = values - pieces[-1].astype(F32)
    return pieces


def grid_rows(kx_first, width):
    lane = lax.broadcasted_iota(jnp.int32, (1, width), 1)
    kx_step = jnp.zeros_like(lane)
    ky = lane
    for edge in range(BOX, width, BOX):
        over = (lane >= edge).astype(jnp.int32)
        ky = ky - BOX * over
        if edge % (2 * BOX) == 0:
            kx_step = kx_step + over
    kx = kx_first + kx_step
    along_y = jnp.minimum(ky, BOX - ky) * 100
    along_x = jnp.minimum(kx, BOX - kx)
    return along_y.astype(F32), along_x.astype(F32)


def gather_tiles(peers, mine_ref, all_ref, sems):
    doms, orients, shells = peers
    z_send, z_recv, x_send, x_recv, c_send, c_recv = sems
    dom = lax.axis_index("dom")
    orient = lax.axis_index("orient")
    shell = lax.axis_index("shell")
    rows = mine_ref.shape[0]
    piece = rows // (orients * shells)
    z_peers = [lax.rem(dom + r, doms) for r in range(1, doms)]
    x_peers = [lax.rem(orient + r, orients) for r in range(1, orients)]
    c_peers = [lax.rem(shell + r, shells) for r in range(1, shells)]

    def part(block, x, c):
        start = pl.multiple_of(block * rows + (x * shells + c) * piece, 16)
        return all_ref.at[pl.ds(start, piece)]

    first = pl.multiple_of((orient * shells + shell) * piece, 16)
    started = []

    def send(source, target, send_sem, recv_sem, device):
        copy = pltpu.make_async_remote_copy(
            src_ref=source,
            dst_ref=target,
            send_sem=send_sem,
            recv_sem=recv_sem,
            device_id=device,
            device_id_type=MESH,
        )
        copy.start()
        started.append(copy)

    def arrived(target, send_sem, recv_sem, device):
        pltpu.make_async_remote_copy(
            src_ref=target,
            dst_ref=target,
            send_sem=send_sem,
            recv_sem=recv_sem,
            device_id=device,
            device_id_type=MESH,
        ).wait_recv()

    for r, z in enumerate(z_peers):
        send(
            mine_ref.at[pl.ds(first, piece)],
            part(dom, orient, shell),
            z_send.at[r],
            z_recv.at[dom],
            {"dom": z},
        )
    yield None
    for r, z in enumerate(z_peers):
        held = part(z, orient, shell)
        arrived(held, z_send.at[r], z_recv.at[z], {"dom": z})
        for i, x in enumerate(x_peers):
            send(held, held, x_send.at[r, i], x_recv.at[z, orient], {"orient": x})
        for i, c in enumerate(c_peers):
            send(held, held, c_send.at[r, 0, i], c_recv.at[z, orient, shell], {"shell": c})
    for r, z in enumerate(z_peers):
        for k, x in enumerate(x_peers):
            held = part(z, x, shell)
            arrived(held, x_send.at[r, k], x_recv.at[z, x], {"orient": x})
            for i, c in enumerate(c_peers):
                send(held, held, c_send.at[r, 1 + k, i], c_recv.at[z, x, shell], {"shell": c})
    for r, z in enumerate(z_peers):
        for k in range(orients):
            x = lax.rem(orient + k, orients)
            for i, c in enumerate(c_peers):
                arrived(part(z, x, c), c_send.at[r, k, i], c_recv.at[z, x, c], {"shell": c})
        yield z
    for copy in started:
        copy.wait_send()


def assign_kernel(
    peers,
    sub_rows,
    owned,
    code_ref,
    slope_ref,
    mine_ref,
    x_ref,
    y_ref,
    rot_ref,
    weighted_ref,
    weights_ref,
    hot_ref,
    tiles_ref,
    tile_t,
    x_tab,
    held,
    slopes,
    tomos,
    partial_ref,
    scores,
    outgoing,
    z_send,
    z_recv,
    x_send,
    x_recv,
    c_send,
    c_recv,
    s_send,
    s_recv,
    w_send,
    w_recv,
):
    doms, orients, shells = peers
    count = doms * orients * shells
    dom = lax.axis_index("dom")
    orient = lax.axis_index("orient")
    shell = lax.axis_index("shell")
    me = (dom * orients + orient) * shells + shell
    position = dom * shells + shell
    barrier = pltpu.get_barrier_semaphore()

    def device(index):
        return {
            "dom": index // (orients * shells),
            "orient": (index // shells) % orients,
            "shell": index % shells,
        }

    def each(body):
        @pl.loop(1, count)
        def _(step):
            body(lax.rem(me + step, count))

    def remote(source, target, send_sem, recv_sem, index):
        return pltpu.make_async_remote_copy(
            src_ref=source,
            dst_ref=target,
            send_sem=send_sem,
            recv_sem=recv_sem,
            device_id=device(index),
            device_id_type=MESH,
        )

    each(lambda j: pl.semaphore_signal(barrier, inc=1, device_id=device(j), device_id_type=MESH))
    pl.semaphore_wait(barrier, count - 1)

    side = tile_t.shape[1]
    tile_dev = mine_ref.shape[0] // side
    gather = gather_tiles(
        peers, mine_ref, tiles_ref, (z_send, z_recv, x_send, x_recv, c_send, c_recv)
    )
    next(gather)

    rows = x_ref.shape[1]
    particles = slopes.shape[0]
    base = x_ref[position]
    for shift in range(x_tab.shape[0]):
        moved = base if shift == 0 else pltpu.roll(base, shift, 1)
        pieces = [piece.astype(F32) for piece in split(moved)]
        filler = x_tab.shape[1] - 3 * rows
        if filler:
            pieces.append(jnp.zeros((filler, LANES), F32))
        x_tab[shift] = jnp.concatenate(pieces, axis=0).astype(BF16)

    @pl.loop(0, tile_dev)
    def _(tile):
        own = mine_ref[pl.ds(pl.multiple_of(tile * side, side), side), :]
        tile_t[dom * tile_dev + tile] = own.astype(F32).T.astype(BF16)

    for block in gather:

        @pl.loop(0, tile_dev)
        def _(tile):
            index = block * tile_dev + tile
            own = tiles_ref[pl.ds(pl.multiple_of(index * side, side), side), :]
            tile_t[index] = own.astype(F32).T.astype(BF16)

    unroll = 8

    @pl.loop(0, particles // unroll)
    def _(step):
        for part in range(unroll):
            particle = step * unroll + part
            code = code_ref[particle]
            tile = code >> 12
            start_y = (code >> 6) & 63
            start_x = code & 63
            both = jnp.dot(x_tab[start_x], tile_t[tile], preferred_element_type=F32)
            along = both[:rows] + (both[rows : 2 * rows] + both[2 * rows : 3 * rows])
            along = pltpu.roll(along, (LANES - start_y) & (LANES - 1), 1)
            held[pl.ds(pl.multiple_of(particle * rows, 8), rows), :] = along
            tomo = tile & (TOMOS - 1)
            slope = slope_ref[tomo].astype(F32)
            slopes[pl.ds(particle, 1), :] = jnp.full((1, LANES), slope, F32)
            tomos[pl.ds(particle, 1), :] = jnp.full((1, LANES), tomo, jnp.int32)

    lane = lax.broadcasted_iota(jnp.int32, tomos.shape, 1)
    hot_ref[...] = jnp.where(tomos[...] == lane, 1.0, 0.0).astype(BF16)
    kx_first = position * sub_rows
    share = scores.shape[1]
    chunk = 256

    @pl.loop(0, particles // chunk)
    def _(block):
        first = pl.multiple_of(block * chunk, chunk)
        own_slope = slopes[pl.ds(first, chunk), :][:, :1]

        def lines(row, which):
            real = held[pl.ds(first * rows + row, chunk, stride=rows), :]
            imag = held[pl.ds(first * rows + sub_rows + row, chunk, stride=rows), :]
            high, middle, low = split(jnp.concatenate([real, imag], axis=1))

            def times(piece, table):
                return jnp.dot(piece, y_ref[which, table], preferred_element_type=F32)

            small = times(high, 2) + times(low, 0) + times(middle, 1)
            return times(high, 0) + (times(high, 1) + times(middle, 0) + small)

        for row in range(0, sub_rows, 2):
            even = lines(row, 0)
            if row + 1 < sub_rows:
                odd = lines(row + 1, 1)
                values = jnp.concatenate(
                    [even[:, :LANES], even[:, LANES:] + odd[:, :LANES], odd[:, LANES:]], axis=1
                )
            else:
                values = even[:, : 2 * BOX]
            width = values.shape[1]
            along_y, along_x = grid_rows(kx_first + row, width)
            inside = along_y <= own_slope * along_x
            values = jnp.where(inside, values * (1.0 / BOX), 0.0)
            weighted_ref[pl.ds(first, chunk), row * 2 * BOX : row * 2 * BOX + width] = values.astype(
                BF16
            )
        result = lax.dot_general(
            weighted_ref[pl.ds(first, chunk), :],
            rot_ref[...],
            (((1,), (1,)), ((), ())),
            preferred_element_type=F32,
        )
        pad = partial_ref.shape[2] - owned
        result = jnp.concatenate([result, jnp.zeros((chunk, pad), F32)], axis=1)
        for line in range(chunk // share):
            partial_ref[block * (chunk // share) + line] = result[line * share : (line + 1) * share]

    each(
        lambda j: remote(
            partial_ref.at[j], scores.at[me], s_send.at[j], s_recv.at[me], j
        ).start()
    )
    scores[me] = partial_ref[me]
    each(
        lambda j: remote(
            partial_ref.at[j], scores.at[j], s_send.at[j], s_recv.at[j], j
        ).wait_recv()
    )
    width = scores.shape[2]
    lane = lax.broadcasted_iota(jnp.int32, (share, width), 1)
    real = lane < owned
    halves = []
    for half in range(orients):
        total = jnp.zeros((share, width), F32)
        for block in range(doms):
            for c in range(shells):
                total = total + scores[(block * orients + half) * shells + c]
        halves.append(jnp.where(real, total * (6.0 / BOX), -3e38))
    top = halves[0]
    for half in halves[1:]:
        top = jnp.maximum(top, half)
    row_top = jnp.max(top, axis=1, keepdims=True)
    shifted = [jnp.where(real, jnp.exp(half - row_top), 0.0) for half in halves]
    row_sum = shifted[0]
    for half in shifted[1:]:
        row_sum = row_sum + half
    row_total = jnp.sum(row_sum, axis=1, keepdims=True)
    logz = row_top + jnp.log(row_total)
    for half in range(orients):
        rounded = (shifted[half] / row_total).astype(BF16).astype(F32)
        outgoing[half] = jnp.where(lane == owned, logz, rounded)
    each(
        lambda j: remote(
            outgoing.at[(j // shells) % orients], weights_ref.at[me], w_send.at[j], w_recv.at[me], j
        ).start()
    )
    weights_ref[me] = outgoing[orient]
    each(
        lambda j: remote(
            outgoing.at[(j // shells) % orients], weights_ref.at[j], w_send.at[j], w_recv.at[j], j
        ).wait_recv()
    )

    def finish(j):
        remote(partial_ref.at[j], scores.at[j], s_send.at[j], s_recv.at[j], j).wait_send()
        remote(
            outgoing.at[(j // shells) % orients], weights_ref.at[j], w_send.at[j], w_recv.at[j], j
        ).wait_send()

    each(finish)


def assign(code, wedge_slope, tiles, rot_ref, peers):
    doms, orients, shells = peers
    count = doms * orients * shells
    tile_dev, side, _ = tiles.shape
    sub_rows = BOX // (doms * shells)
    rows = round_up(2 * sub_rows, 8)
    shifts = side - BOX + 1
    angle = 2.0 * math.pi / BOX
    kx = np.arange(BOX)
    phase = angle * ((kx[:, None] * kx[None, :]) % BOX)
    x_table = np.zeros((doms * shells, rows, LANES), np.float32)
    for position in range(doms * shells):
        own = slice(position * sub_rows, (position + 1) * sub_rows)
        x_table[position, :sub_rows, :BOX] = np.cos(phase[own])
        x_table[position, sub_rows : 2 * sub_rows, :BOX] = -np.sin(phase[own])
    y_real = np.zeros((2 * LANES, 2 * BOX), np.float32)
    y_real[:BOX, :BOX] = np.cos(phase)
    y_real[:BOX, BOX:] = -np.sin(phase)
    y_real[LANES : LANES + BOX, :BOX] = np.sin(phase)
    y_real[LANES : LANES + BOX, BOX:] = np.cos(phase)
    gap = 2 * LANES - 2 * BOX
    rest = np.stack([np.pad(y_real, ((0, 0), (0, gap))), np.pad(y_real, ((0, 0), (gap, 0)))])
    y_table = []
    for _ in range(3):
        y_table.append(rest.astype(BF16))
        rest = rest - y_table[-1].astype(np.float32)
    y_table = np.stack(y_table, axis=1)
    particles = code.shape[0]
    owned, depth = rot_ref.shape
    width = round_up(owned + 1, LANES)
    blocks = (count, particles // count, width)
    dma = pltpu.SemaphoreType.DMA
    weighted, weights, hot = pl.pallas_call(
        functools.partial(assign_kernel, peers, sub_rows, owned),
        out_shape=(
            jax.ShapeDtypeStruct((particles, depth), BF16),
            jax.ShapeDtypeStruct(blocks, F32),
            jax.ShapeDtypeStruct((particles, LANES), BF16),
        ),
        in_specs=[SMEM, SMEM, VMEM, VMEM, VMEM, VMEM],
        out_specs=(VMEM, VMEM, VMEM),
        scratch_shapes=[
            pltpu.VMEM((doms * tile_dev * side, side), BF16),
            pltpu.VMEM((doms * tile_dev, side, side), BF16),
            pltpu.VMEM((shifts, round_up(3 * rows, 16), LANES), BF16),
            pltpu.VMEM((particles * rows, LANES), F32),
            pltpu.VMEM((particles, LANES), F32),
            pltpu.VMEM((particles, LANES), jnp.int32),
            pltpu.VMEM(blocks, F32),
            pltpu.VMEM(blocks, F32),
            pltpu.VMEM((orients,) + blocks[1:], F32),
            dma((doms,)),
            dma((doms,)),
            dma((doms, orients)),
            dma((doms, orients)),
            dma((doms, orients, shells)),
            dma((doms, orients, shells)),
            dma((count,)),
            dma((count,)),
            dma((count,)),
            dma((count,)),
        ],
        compiler_params=pltpu.CompilerParams(
            collective_id=0, has_side_effects=True, vmem_limit_bytes=LIMIT
        ),
        name="assign",
    )(code, wedge_slope, tiles.reshape(tile_dev * side, side), x_table, y_table, rot_ref)
    return weighted, weights.reshape(particles, width), hot


def average_kernel(
    sub_rows, shells, owned, slope_ref, weights_ref, weighted_ref, hot_ref, out_ref, logz_ref
):
    dom = lax.axis_index("dom")
    position = dom * shells + lax.axis_index("shell")
    turned = weights_ref[...].T
    part_dev = logz_ref.shape[1]
    particles = turned.shape[1]
    logz_row = jnp.broadcast_to(turned[owned : owned + 1], (8, particles))
    logz_ref[...] = pltpu.roll(logz_row, lax.rem(particles - dom * part_dev, particles), 1)[
        :1, :part_dev
    ]
    kept = turned[:owned].astype(BF16)
    tomo_weight = jnp.dot(kept, hot_ref[...], preferred_element_type=F32)[:, :TOMOS]
    pieces = []
    rest = tomo_weight
    for _ in range(3):
        piece = rest.astype(BF16)
        pieces.append(piece.astype(F32))
        rest = rest - pieces[-1]
    pieces = jnp.concatenate(pieces, axis=1).astype(BF16)
    tomo_row = lax.broadcasted_iota(jnp.int32, (TOMOS, 1), 0)
    slopes = jnp.zeros((TOMOS, 1), F32)
    for tomo in range(TOMOS):
        slopes = jnp.where(tomo_row == tomo, slope_ref[tomo].astype(F32), slopes)
    for row in range(0, sub_rows, 2):
        width = min(2, sub_rows - row) * 2 * BOX
        along_y, along_x = grid_rows(position * sub_rows + row, width)
        wedge = jnp.where(along_y <= slopes * along_x, 1.0, 0.0)
        wedge = jnp.concatenate([wedge, wedge, wedge], axis=0).astype(BF16)
        span = slice(row * 2 * BOX, row * 2 * BOX + width)
        numerator = jnp.dot(kept, weighted_ref[:, span], preferred_element_type=F32)
        denominator = jnp.dot(pieces, wedge, preferred_element_type=F32)
        out_ref[:, span] = numerator / (denominator + 1.0)


def average(wedge_slope, weights, weighted, hot, owned, doms, shells):
    part_dev = weights.shape[0] // doms
    return pl.pallas_call(
        functools.partial(average_kernel, BOX // (doms * shells), shells, owned),
        out_shape=(
            jax.ShapeDtypeStruct((owned, weighted.shape[1]), F32),
            jax.ShapeDtypeStruct((1, part_dev), F32),
        ),
        in_specs=[SMEM, VMEM, VMEM, VMEM],
        out_specs=(VMEM, VMEM),
        compiler_params=pltpu.CompilerParams(vmem_limit_bytes=LIMIT),
        name="average",
    )(wedge_slope, weights, weighted, hot)


def local(tiles, particle_tile, particle_offset, wedge_slope, rot_ref):
    doms = lax.axis_size("dom")
    orients = lax.axis_size("orient")
    shells = lax.axis_size("shell")
    packing = jnp.array([64, 1], jnp.int32)
    code = particle_tile * 4096 + jnp.sum(particle_offset * packing[None, :], axis=1)
    weighted, weights, hot = assign(code, wedge_slope, tiles, rot_ref, (doms, orients, shells))
    owned = rot_ref.shape[0]
    new_reference, logz = average(wedge_slope, weights, weighted, hot, owned, doms, shells)
    return new_reference, logz.reshape(-1)


def solution(mesh):
    in_specs = (
        P(("groups", "dom"), None, None),
        P("groups"),
        P("groups", None),
        P("groups"),
        P(("groups", "orient"), ("dom", "shell")),
    )
    out_specs = (P(("groups", "orient"), ("dom", "shell")), P(("groups", "dom")))
    return jax.shard_map(local, mesh=mesh, in_specs=in_specs, out_specs=out_specs, check_vma=False)
```

```python
import functools
import math

import jax
import jax.numpy as jnp
import numpy as np
from jax import lax
from jax.experimental import pallas as pl
from jax.experimental.pallas import tpu as pltpu
from jax.sharding import PartitionSpec as P

BOX = 96
TOMOS = 16
LANES = 128
MESH = pl.DeviceIdType.MESH
VMEM = pl.BlockSpec(memory_space=pltpu.VMEM)
ANY = pl.BlockSpec(memory_space=pl.ANY)
SMEM = pl.BlockSpec(memory_space=pltpu.SMEM)
F32 = jnp.float32
BF16 = jnp.bfloat16
LIMIT = 56 * 1024 * 1024


def round_up(value, step):
    return -(-value // step) * step


def split(values):
    pieces = []
    for _ in range(3):
        pieces.append(values.astype(BF16))
        values = values - pieces[-1].astype(F32)
    return pieces


def grid_rows(kx_first, width):
    lane = lax.broadcasted_iota(jnp.int32, (1, width), 1)
    kx_step = jnp.zeros_like(lane)
    ky = lane
    for edge in range(BOX, width, BOX):
        over = (lane >= edge).astype(jnp.int32)
        ky = ky - BOX * over
        if edge % (2 * BOX) == 0:
            kx_step = kx_step + over
    kx = kx_first + kx_step
    along_y = jnp.minimum(ky, BOX - ky) * 100
    along_x = jnp.minimum(kx, BOX - kx)
    return along_y.astype(F32), along_x.astype(F32)


def gather_tiles(peers, mine_ref, all_ref, sems):
    doms, orients, shells = peers
    z_send, z_recv, x_send, x_recv, c_send, c_recv = sems
    dom = lax.axis_index("dom")
    orient = lax.axis_index("orient")
    shell = lax.axis_index("shell")
    rows = mine_ref.shape[0]
    piece = rows // (orients * shells)
    z_peers = [lax.rem(dom + r, doms) for r in range(1, doms)]
    x_peers = [lax.rem(orient + r, orients) for r in range(1, orients)]
    c_peers = [lax.rem(shell + r, shells) for r in range(1, shells)]

    def part(block, x, c):
        start = pl.multiple_of(block * rows + (x * shells + c) * piece, 16)
        return all_ref.at[pl.ds(start, piece)]

    first = pl.multiple_of((orient * shells + shell) * piece, 16)
    started = []

    def send(source, target, send_sem, recv_sem, device):
        copy = pltpu.make_async_remote_copy(
            src_ref=source,
            dst_ref=target,
            send_sem=send_sem,
            recv_sem=recv_sem,
            device_id=device,
            device_id_type=MESH,
        )
        copy.start()
        started.append(copy)

    def arrived(target, send_sem, recv_sem, device):
        pltpu.make_async_remote_copy(
            src_ref=target,
            dst_ref=target,
            send_sem=send_sem,
            recv_sem=recv_sem,
            device_id=device,
            device_id_type=MESH,
        ).wait_recv()

    for r, z in enumerate(z_peers):
        send(
            mine_ref.at[pl.ds(first, piece)],
            part(dom, orient, shell),
            z_send.at[r],
            z_recv.at[dom],
            {"dom": z},
        )
    yield None
    for r, z in enumerate(z_peers):
        held = part(z, orient, shell)
        arrived(held, z_send.at[r], z_recv.at[z], {"dom": z})
        for i, x in enumerate(x_peers):
            send(held, held, x_send.at[r, i], x_recv.at[z, orient], {"orient": x})
        for i, c in enumerate(c_peers):
            send(held, held, c_send.at[r, 0, i], c_recv.at[z, orient, shell], {"shell": c})
    for r, z in enumerate(z_peers):
        for k, x in enumerate(x_peers):
            held = part(z, x, shell)
            arrived(held, x_send.at[r, k], x_recv.at[z, x], {"orient": x})
            for i, c in enumerate(c_peers):
                send(held, held, c_send.at[r, 1 + k, i], c_recv.at[z, x, shell], {"shell": c})
    for r, z in enumerate(z_peers):
        for k in range(orients):
            x = lax.rem(orient + k, orients)
            for i, c in enumerate(c_peers):
                arrived(part(z, x, c), c_send.at[r, k, i], c_recv.at[z, x, c], {"shell": c})
        yield z
    for copy in started:
        copy.wait_send()


def assign_kernel(
    peers,
    sub_rows,
    owned,
    tile_ref,
    offset_ref,
    slope_ref,
    mine_ref,
    x_ref,
    y_hbm,
    rot_hbm,
    weighted_hbm,
    weights_ref,
    hot_ref,
    y_ref,
    rot_ref,
    weighted_ref,
    l_sem,
    tiles_ref,
    tile_t,
    x_tab,
    held,
    slopes,
    tomos,
    partial_ref,
    scores,
    outgoing,
    z_send,
    z_recv,
    x_send,
    x_recv,
    c_send,
    c_recv,
    s_send,
    s_recv,
    w_send,
    w_recv,
):
    doms, orients, shells = peers
    count = doms * orients * shells
    dom = lax.axis_index("dom")
    orient = lax.axis_index("orient")
    shell = lax.axis_index("shell")
    me = (dom * orients + orient) * shells + shell
    position = dom * shells + shell
    barrier = pltpu.get_barrier_semaphore()

    def near(z, skip):
        found = []
        for x in range(orients):
            for c in range(shells):
                if skip and x == 0 and c == 0:
                    continue
                found.append((z, lax.rem(orient + x, orients), lax.rem(shell + c, shells)))
        return found

    def each(body):
        if doms > 4:

            @pl.loop(1, doms)
            def _(step):
                for peer in near(lax.rem(dom + step, doms), False):
                    body(peer)

        else:
            for step in range(1, doms):
                for peer in near(lax.rem(dom + step, doms), False):
                    body(peer)
        for peer in near(dom, True):
            body(peer)

    def number(peer):
        return (peer[0] * orients + peer[1]) * shells + peer[2]

    def device(peer):
        return {"dom": peer[0], "orient": peer[1], "shell": peer[2]}

    def remote(source, target, send_sem, recv_sem, peer):
        return pltpu.make_async_remote_copy(
            src_ref=source,
            dst_ref=target,
            send_sem=send_sem,
            recv_sem=recv_sem,
            device_id=device(peer),
            device_id_type=MESH,
        )

    def part_copy(peer, slot):
        j = number(peer)
        return remote(partial_ref.at[j], scores.at[slot], s_send.at[j], s_recv.at[slot], peer)

    def weight_copy(peer, slot):
        j = number(peer)
        return remote(
            outgoing.at[peer[1]], weights_ref.at[slot], w_send.at[j], w_recv.at[slot], peer
        )

    each(lambda j: pl.semaphore_signal(barrier, inc=1, device_id=device(j), device_id_type=MESH))
    y_copy = pltpu.make_async_copy(y_hbm, y_ref, l_sem.at[0])
    rot_copy = pltpu.make_async_copy(rot_hbm, rot_ref, l_sem.at[1])
    y_copy.start()
    rot_copy.start()
    pl.semaphore_wait(barrier, count - 1)

    side = tile_t.shape[1]
    tile_dev = mine_ref.shape[0] // side
    gather = gather_tiles(
        peers, mine_ref, tiles_ref, (z_send, z_recv, x_send, x_recv, c_send, c_recv)
    )
    next(gather)

    rows = x_ref.shape[1]
    particles = slopes.shape[0]
    base = x_ref[position]
    for shift in range(x_tab.shape[0]):
        moved = base if shift == 0 else pltpu.roll(base, shift, 1)
        pieces = [piece.astype(F32) for piece in split(moved)]
        filler = x_tab.shape[1] - 3 * rows
        if filler:
            pieces.append(jnp.zeros((filler, LANES), F32))
        x_tab[shift] = jnp.concatenate(pieces, axis=0).astype(BF16)

    @pl.loop(0, tile_dev)
    def _(tile):
        own = mine_ref[pl.ds(pl.multiple_of(tile * side, side), side), :]
        tile_t[dom * tile_dev + tile] = own.astype(F32).T.astype(BF16)

    for block in gather:

        @pl.loop(0, tile_dev)
        def _(tile):
            index = block * tile_dev + tile
            own = tiles_ref[pl.ds(pl.multiple_of(index * side, side), side), :]
            tile_t[index] = own.astype(F32).T.astype(BF16)

    unroll = 16

    @pl.loop(0, particles // unroll)
    def _(step):
        for part in range(unroll):
            particle = step * unroll + part
            tile = tile_ref[particle]
            start_y = offset_ref[0, particle]
            start_x = offset_ref[1, particle]
            both = jnp.dot(x_tab[start_x], tile_t[tile], preferred_element_type=F32)
            along = both[:rows] + (both[rows : 2 * rows] + both[2 * rows : 3 * rows])
            along = pltpu.roll(along, (LANES - start_y) & (LANES - 1), 1)
            held[pl.ds(pl.multiple_of(particle * rows, 8), rows), :] = along
            tomo = tile & (TOMOS - 1)
            slope = slope_ref[tomo].astype(F32)
            slopes[pl.ds(particle, 1), :] = jnp.full((1, LANES), slope, F32)
            tomos[pl.ds(particle, 1), :] = jnp.full((1, LANES), tomo, jnp.int32)

    y_copy.wait()
    rot_copy.wait()
    lane = lax.broadcasted_iota(jnp.int32, tomos.shape, 1)
    hot_ref[...] = jnp.where(tomos[...] == lane, 1.0, 0.0).astype(BF16)
    kx_first = position * sub_rows
    share = scores.shape[1]
    chunk = 256

    @pl.loop(0, particles // chunk)
    def _(block):
        first = pl.multiple_of(block * chunk, chunk)
        own_slope = slopes[pl.ds(first, chunk), :][:, :1]

        def lines(row, which):
            real = held[pl.ds(first * rows + row, chunk, stride=rows), :]
            imag = held[pl.ds(first * rows + sub_rows + row, chunk, stride=rows), :]
            high, middle, low = split(jnp.concatenate([real, imag], axis=1))

            def times(piece, table):
                return jnp.dot(piece, y_ref[which, table], preferred_element_type=F32)

            small = times(high, 2) + times(low, 0) + times(middle, 1)
            return times(high, 0) + (times(high, 1) + times(middle, 0) + small)

        for row in range(0, sub_rows, 2):
            even = lines(row, 0)
            if row + 1 < sub_rows:
                odd = lines(row + 1, 1)
                values = jnp.concatenate(
                    [even[:, :LANES], even[:, LANES:] + odd[:, :LANES], odd[:, LANES:]], axis=1
                )
            else:
                values = even[:, : 2 * BOX]
            width = values.shape[1]
            along_y, along_x = grid_rows(kx_first + row, width)
            inside = along_y <= own_slope * along_x
            values = jnp.where(inside, values * (1.0 / BOX), 0.0)
            weighted_ref[pl.ds(first, chunk), row * 2 * BOX : row * 2 * BOX + width] = values.astype(
                BF16
            )
        result = lax.dot_general(
            weighted_ref[pl.ds(first, chunk), :],
            rot_ref[...],
            (((1,), (1,)), ((), ())),
            preferred_element_type=F32,
        )
        pad = partial_ref.shape[2] - owned
        result = jnp.concatenate([result, jnp.zeros((chunk, pad), F32)], axis=1)
        for line in range(chunk // share):
            partial_ref[block * (chunk // share) + line] = result[line * share : (line + 1) * share]

    out_copy = pltpu.make_async_copy(weighted_ref, weighted_hbm, l_sem.at[2])
    each(lambda peer: part_copy(peer, me).start())
    out_copy.start()
    scores[me] = partial_ref[me]
    each(lambda peer: part_copy(peer, number(peer)).wait_recv())
    width = scores.shape[2]
    lane = lax.broadcasted_iota(jnp.int32, (share, width), 1)
    real = lane < owned
    halves = []
    for half in range(orients):
        total = jnp.zeros((share, width), F32)
        for block in range(doms):
            for c in range(shells):
                total = total + scores[(block * orients + half) * shells + c]
        halves.append(jnp.where(real, total * (6.0 / BOX), -3e38))
    top = halves[0]
    for half in halves[1:]:
        top = jnp.maximum(top, half)
    row_top = jnp.max(top, axis=1, keepdims=True)
    shifted = [jnp.where(real, jnp.exp(half - row_top), 0.0) for half in halves]
    row_sum = shifted[0]
    for half in shifted[1:]:
        row_sum = row_sum + half
    row_total = jnp.sum(row_sum, axis=1, keepdims=True)
    logz = row_top + jnp.log(row_total)
    for half in range(orients):
        rounded = (shifted[half] / row_total).astype(BF16).astype(F32)
        outgoing[half] = jnp.where(lane == owned, logz, rounded)
    each(lambda peer: weight_copy(peer, me).start())
    weights_ref[me] = outgoing[orient]
    out_copy.wait()

    def finish(peer):
        part_copy(peer, me).wait_send()
        weight_copy(peer, me).wait_send()

    each(lambda peer: weight_copy(peer, number(peer)).wait_recv())
    each(finish)


def assign(particle_tile, particle_offset, wedge_slope, tiles, rot_ref, peers):
    doms, orients, shells = peers
    count = doms * orients * shells
    tile_dev, side, _ = tiles.shape
    sub_rows = BOX // (doms * shells)
    rows = round_up(2 * sub_rows, 8)
    shifts = side - BOX + 1
    angle = 2.0 * math.pi / BOX
    kx = np.arange(BOX)
    phase = angle * ((kx[:, None] * kx[None, :]) % BOX)
    x_table = np.zeros((doms * shells, rows, LANES), np.float32)
    for position in range(doms * shells):
        own = slice(position * sub_rows, (position + 1) * sub_rows)
        x_table[position, :sub_rows, :BOX] = np.cos(phase[own])
        x_table[position, sub_rows : 2 * sub_rows, :BOX] = -np.sin(phase[own])
    y_real = np.zeros((2 * LANES, 2 * BOX), np.float32)
    y_real[:BOX, :BOX] = np.cos(phase)
    y_real[:BOX, BOX:] = -np.sin(phase)
    y_real[LANES : LANES + BOX, :BOX] = np.sin(phase)
    y_real[LANES : LANES + BOX, BOX:] = np.cos(phase)
    gap = 2 * LANES - 2 * BOX
    rest = np.stack([np.pad(y_real, ((0, 0), (0, gap))), np.pad(y_real, ((0, 0), (gap, 0)))])
    y_table = []
    for _ in range(3):
        y_table.append(rest.astype(BF16))
        rest = rest - y_table[-1].astype(np.float32)
    y_table = np.stack(y_table, axis=1)
    particles = particle_tile.shape[0]
    owned, depth = rot_ref.shape
    width = round_up(owned + 1, LANES)
    blocks = (count, particles // count, width)
    dma = pltpu.SemaphoreType.DMA
    weighted, weights, hot = pl.pallas_call(
        functools.partial(assign_kernel, peers, sub_rows, owned),
        out_shape=(
            jax.ShapeDtypeStruct((particles, depth), BF16),
            jax.ShapeDtypeStruct(blocks, F32),
            jax.ShapeDtypeStruct((particles, LANES), BF16),
        ),
        in_specs=[SMEM, SMEM, SMEM, VMEM, VMEM, ANY, ANY],
        out_specs=(ANY, VMEM, VMEM),
        scratch_shapes=[
            pltpu.VMEM(y_table.shape, BF16),
            pltpu.VMEM(rot_ref.shape, BF16),
            pltpu.VMEM((particles, depth), BF16),
            dma((3,)),
            pltpu.VMEM((doms * tile_dev * side, side), BF16),
            pltpu.VMEM((doms * tile_dev, side, side), BF16),
            pltpu.VMEM((shifts, round_up(3 * rows, 16), LANES), BF16),
            pltpu.VMEM((particles * rows, LANES), F32),
            pltpu.VMEM((particles, LANES), F32),
            pltpu.VMEM((particles, LANES), jnp.int32),
            pltpu.VMEM(blocks, F32),
            pltpu.VMEM(blocks, F32),
            pltpu.VMEM((orients,) + blocks[1:], F32),
            dma((doms,)),
            dma((doms,)),
            dma((doms, orients)),
            dma((doms, orients)),
            dma((doms, orients, shells)),
            dma((doms, orients, shells)),
            dma((count,)),
            dma((count,)),
            dma((count,)),
            dma((count,)),
        ],
        compiler_params=pltpu.CompilerParams(
            collective_id=0, has_side_effects=True, vmem_limit_bytes=LIMIT
        ),
        name="assign",
    )(particle_tile, particle_offset.T, wedge_slope, tiles.reshape(tile_dev * side, side), x_table, y_table, rot_ref)
    return weighted, weights.reshape(particles, width), hot


def average_kernel(
    sub_rows, shells, owned, slope_ref, weights_ref, weighted_ref, hot_ref, out_ref, logz_ref
):
    dom = lax.axis_index("dom")
    position = dom * shells + lax.axis_index("shell")
    turned = weights_ref[...].T
    part_dev = logz_ref.shape[1]
    particles = turned.shape[1]
    logz_row = jnp.broadcast_to(turned[owned : owned + 1], (8, particles))
    logz_ref[...] = pltpu.roll(logz_row, lax.rem(particles - dom * part_dev, particles), 1)[
        :1, :part_dev
    ]
    kept = turned[:owned].astype(BF16)
    tomo_weight = jnp.dot(kept, hot_ref[...], preferred_element_type=F32)[:, :TOMOS]
    pieces = []
    rest = tomo_weight
    for _ in range(3):
        piece = rest.astype(BF16)
        pieces.append(piece.astype(F32))
        rest = rest - pieces[-1]
    pieces = jnp.concatenate(pieces, axis=1).astype(BF16)
    tomo_row = lax.broadcasted_iota(jnp.int32, (TOMOS, 1), 0)
    slopes = jnp.zeros((TOMOS, 1), F32)
    for tomo in range(TOMOS):
        slopes = jnp.where(tomo_row == tomo, slope_ref[tomo].astype(F32), slopes)
    for row in range(0, sub_rows, 2):
        width = min(2, sub_rows - row) * 2 * BOX
        along_y, along_x = grid_rows(position * sub_rows + row, width)
        wedge = jnp.where(along_y <= slopes * along_x, 1.0, 0.0)
        wedge = jnp.concatenate([wedge, wedge, wedge], axis=0).astype(BF16)
        span = slice(row * 2 * BOX, row * 2 * BOX + width)
        numerator = jnp.dot(kept, weighted_ref[:, span], preferred_element_type=F32)
        denominator = jnp.dot(pieces, wedge, preferred_element_type=F32)
        out_ref[:, span] = numerator / (denominator + 1.0)


def average(wedge_slope, weights, weighted, hot, owned, doms, shells):
    part_dev = weights.shape[0] // doms
    return pl.pallas_call(
        functools.partial(average_kernel, BOX // (doms * shells), shells, owned),
        out_shape=(
            jax.ShapeDtypeStruct((owned, weighted.shape[1]), F32),
            jax.ShapeDtypeStruct((1, part_dev), F32),
        ),
        in_specs=[SMEM, VMEM, VMEM, VMEM],
        out_specs=(VMEM, VMEM),
        compiler_params=pltpu.CompilerParams(vmem_limit_bytes=LIMIT),
        name="average",
    )(wedge_slope, weights, weighted, hot)


def local(tiles, particle_tile, particle_offset, wedge_slope, rot_ref):
    doms = lax.axis_size("dom")
    orients = lax.axis_size("orient")
    shells = lax.axis_size("shell")
    weighted, weights, hot = assign(
        particle_tile, particle_offset, wedge_slope, tiles, rot_ref, (doms, orients, shells)
    )
    owned = rot_ref.shape[0]
    new_reference, logz = average(wedge_slope, weights, weighted, hot, owned, doms, shells)
    return new_reference, logz.reshape(-1)


def solution(mesh):
    in_specs = (
        P(("groups", "dom"), None, None),
        P("groups"),
        P("groups", None),
        P("groups"),
        P(("groups", "orient"), ("dom", "shell")),
    )
    out_specs = (P(("groups", "orient"), ("dom", "shell")), P(("groups", "dom")))
    return jax.shard_map(local, mesh=mesh, in_specs=in_specs, out_specs=out_specs, check_vma=False)
```

```python
import functools
import math

import jax
import jax.numpy as jnp
import numpy as np
from jax import lax
from jax.experimental import pallas as pl
from jax.experimental.pallas import tpu as pltpu
from jax.sharding import PartitionSpec as P

BOX = 96
TOMOS = 16
LANES = 128
MESH = pl.DeviceIdType.MESH
VMEM = pl.BlockSpec(memory_space=pltpu.VMEM)
ANY = pl.BlockSpec(memory_space=pl.ANY)
SMEM = pl.BlockSpec(memory_space=pltpu.SMEM)
F32 = jnp.float32
BF16 = jnp.bfloat16
LIMIT = 56 * 1024 * 1024


def round_up(value, step):
    return -(-value // step) * step


def split(values):
    pieces = []
    for _ in range(3):
        pieces.append(values.astype(BF16))
        values = values - pieces[-1].astype(F32)
    return pieces


def grid_rows(kx_first, width):
    lane = lax.broadcasted_iota(jnp.int32, (1, width), 1)
    kx_step = jnp.zeros_like(lane)
    ky = lane
    for edge in range(BOX, width, BOX):
        over = (lane >= edge).astype(jnp.int32)
        ky = ky - BOX * over
        if edge % (2 * BOX) == 0:
            kx_step = kx_step + over
    kx = kx_first + kx_step
    along_y = jnp.minimum(ky, BOX - ky) * 100
    along_x = jnp.minimum(kx, BOX - kx)
    return along_y.astype(F32), along_x.astype(F32)


def gather_tiles(peers, mine_ref, all_ref, sems):
    doms, orients, shells = peers
    z_send, z_recv, x_send, x_recv, c_send, c_recv = sems
    dom = lax.axis_index("dom")
    orient = lax.axis_index("orient")
    shell = lax.axis_index("shell")
    rows = mine_ref.shape[0]
    piece = rows // (orients * shells)
    far_first = sorted(range(1, doms), key=lambda r: -min(r, doms - r))
    z_peers = [lax.rem(dom + r, doms) for r in far_first]
    x_peers = [lax.rem(orient + r, orients) for r in range(1, orients)]
    c_peers = [lax.rem(shell + r, shells) for r in range(1, shells)]

    def part(block, x, c):
        start = pl.multiple_of(block * rows + (x * shells + c) * piece, 16)
        return all_ref.at[pl.ds(start, piece)]

    first = pl.multiple_of((orient * shells + shell) * piece, 16)
    started = []

    def send(source, target, send_sem, recv_sem, device):
        copy = pltpu.make_async_remote_copy(
            src_ref=source,
            dst_ref=target,
            send_sem=send_sem,
            recv_sem=recv_sem,
            device_id=device,
            device_id_type=MESH,
        )
        copy.start()
        started.append(copy)

    def arrived(target, send_sem, recv_sem, device):
        pltpu.make_async_remote_copy(
            src_ref=target,
            dst_ref=target,
            send_sem=send_sem,
            recv_sem=recv_sem,
            device_id=device,
            device_id_type=MESH,
        ).wait_recv()

    for r, z in enumerate(z_peers):
        send(
            mine_ref.at[pl.ds(first, piece)],
            part(dom, orient, shell),
            z_send.at[r],
            z_recv.at[dom],
            {"dom": z},
        )
    yield None
    for r, z in enumerate(z_peers):
        held = part(z, orient, shell)
        arrived(held, z_send.at[r], z_recv.at[z], {"dom": z})
        for i, x in enumerate(x_peers):
            send(held, held, x_send.at[r, i], x_recv.at[z, orient], {"orient": x})
        for i, c in enumerate(c_peers):
            send(held, held, c_send.at[r, 0, i], c_recv.at[z, orient, shell], {"shell": c})
    for r, z in enumerate(z_peers):
        for k, x in enumerate(x_peers):
            held = part(z, x, shell)
            arrived(held, x_send.at[r, k], x_recv.at[z, x], {"orient": x})
            for i, c in enumerate(c_peers):
                send(held, held, c_send.at[r, 1 + k, i], c_recv.at[z, x, shell], {"shell": c})
    for r, z in enumerate(z_peers):
        for k in range(orients):
            x = lax.rem(orient + k, orients)
            for i, c in enumerate(c_peers):
                arrived(part(z, x, c), c_send.at[r, k, i], c_recv.at[z, x, c], {"shell": c})
        yield z
    for copy in started:
        copy.wait_send()


def assign_kernel(
    peers,
    sub_rows,
    owned,
    tile_ref,
    offset_ref,
    slope_ref,
    mine_ref,
    x_ref,
    y_hbm,
    rot_hbm,
    weighted_hbm,
    weights_ref,
    logz_ref,
    hot_ref,
    y_ref,
    rot_ref,
    weighted_ref,
    l_sem,
    tiles_ref,
    tile_t,
    x_tab,
    held,
    slopes,
    tomos,
    partial_ref,
    scores,
    outgoing,
    z_send,
    z_recv,
    x_send,
    x_recv,
    c_send,
    c_recv,
    s_send,
    s_recv,
    w_send,
    w_recv,
    g_send,
    g_recv,
):
    doms, orients, shells = peers
    count = doms * orients * shells
    dom = lax.axis_index("dom")
    orient = lax.axis_index("orient")
    shell = lax.axis_index("shell")
    me = (dom * orients + orient) * shells + shell
    position = dom * shells + shell
    barrier = pltpu.get_barrier_semaphore()

    def near(z, skip):
        found = []
        for x in range(orients):
            for c in range(shells):
                if skip and x == 0 and c == 0:
                    continue
                found.append((z, lax.rem(orient + x, orients), lax.rem(shell + c, shells)))
        return found

    def each(body):
        if doms > 4:

            @pl.loop(1, doms)
            def _(step):
                for peer in near(lax.rem(dom + step, doms), False):
                    body(peer)

        else:
            for step in range(1, doms):
                for peer in near(lax.rem(dom + step, doms), False):
                    body(peer)
        for peer in near(dom, True):
            body(peer)

    def number(peer):
        return (peer[0] * orients + peer[1]) * shells + peer[2]

    def device(peer):
        return {"dom": peer[0], "orient": peer[1], "shell": peer[2]}

    def remote(source, target, send_sem, recv_sem, peer):
        return pltpu.make_async_remote_copy(
            src_ref=source,
            dst_ref=target,
            send_sem=send_sem,
            recv_sem=recv_sem,
            device_id=device(peer),
            device_id_type=MESH,
        )

    def part_copy(peer, slot):
        j = number(peer)
        return remote(partial_ref.at[j], scores.at[slot], s_send.at[j], s_recv.at[slot], peer)

    def weight_copy(peer, slot):
        j = number(peer)
        return remote(
            outgoing.at[peer[1]], weights_ref.at[slot], w_send.at[j], w_recv.at[slot], peer
        )

    def logz_copy(peer, slot):
        q = peer[1] * shells + peer[2]
        block = logz_ref.at[slot]
        return remote(block, block, g_send.at[q], g_recv.at[slot], peer)

    each(lambda j: pl.semaphore_signal(barrier, inc=1, device_id=device(j), device_id_type=MESH))
    y_copy = pltpu.make_async_copy(y_hbm, y_ref, l_sem.at[0])
    rot_copy = pltpu.make_async_copy(rot_hbm, rot_ref, l_sem.at[1])
    y_copy.start()
    rot_copy.start()
    pl.semaphore_wait(barrier, count - 1)

    side = tile_t.shape[1]
    tile_dev = mine_ref.shape[0] // side
    gather = gather_tiles(
        peers, mine_ref, tiles_ref, (z_send, z_recv, x_send, x_recv, c_send, c_recv)
    )
    next(gather)

    rows = x_ref.shape[1]
    particles = slopes.shape[0]
    base = x_ref[position]
    for shift in range(x_tab.shape[0]):
        moved = base if shift == 0 else pltpu.roll(base, shift, 1)
        pieces = [piece.astype(F32) for piece in split(moved)]
        filler = x_tab.shape[1] - 3 * rows
        if filler:
            pieces.append(jnp.zeros((filler, LANES), F32))
        x_tab[shift] = jnp.concatenate(pieces, axis=0).astype(BF16)

    @pl.loop(0, tile_dev)
    def _(tile):
        own = mine_ref[pl.ds(pl.multiple_of(tile * side, side), side), :]
        tile_t[dom * tile_dev + tile] = own.astype(F32).T.astype(BF16)

    for block in gather:

        @pl.loop(0, tile_dev)
        def _(tile):
            index = block * tile_dev + tile
            own = tiles_ref[pl.ds(pl.multiple_of(index * side, side), side), :]
            tile_t[index] = own.astype(F32).T.astype(BF16)

    unroll = 64

    @pl.loop(0, particles // unroll)
    def _(step):
        for part in range(unroll):
            particle = step * unroll + part
            tile = tile_ref[particle]
            start_y = offset_ref[0, particle]
            start_x = offset_ref[1, particle]
            both = jnp.dot(x_tab[start_x], tile_t[tile], preferred_element_type=F32)
            along = both[:rows] + (both[rows : 2 * rows] + both[2 * rows : 3 * rows])
            along = pltpu.roll(along, (LANES - start_y) & (LANES - 1), 1)
            held[pl.ds(pl.multiple_of(particle * rows, 8), rows), :] = along
            tomo = tile & (TOMOS - 1)
            slope = slope_ref[tomo].astype(F32)
            slopes[pl.ds(particle, 1), :] = jnp.full((1, LANES), slope, F32)
            tomos[pl.ds(particle, 1), :] = jnp.full((1, LANES), tomo, jnp.int32)

    y_copy.wait()
    rot_copy.wait()
    lane = lax.broadcasted_iota(jnp.int32, tomos.shape, 1)
    hot_ref[...] = jnp.where(tomos[...] == lane, 1.0, 0.0).astype(BF16)
    kx_first = position * sub_rows
    share = scores.shape[1]
    chunk = 256

    @pl.loop(0, particles // chunk)
    def _(block):
        first = pl.multiple_of(block * chunk, chunk)
        own_slope = slopes[pl.ds(first, chunk), :][:, :1]

        def lines(row, which):
            real = held[pl.ds(first * rows + row, chunk, stride=rows), :]
            imag = held[pl.ds(first * rows + sub_rows + row, chunk, stride=rows), :]
            high, middle, low = split(jnp.concatenate([real, imag], axis=1))

            def times(piece, table):
                return jnp.dot(piece, y_ref[which, table], preferred_element_type=F32)

            small = times(high, 2) + times(low, 0) + times(middle, 1)
            return times(high, 0) + (times(high, 1) + times(middle, 0) + small)

        for row in range(0, sub_rows, 2):
            even = lines(row, 0)
            if row + 1 < sub_rows:
                odd = lines(row + 1, 1)
                values = jnp.concatenate(
                    [even[:, :LANES], even[:, LANES:] + odd[:, :LANES], odd[:, LANES:]], axis=1
                )
            else:
                values = even[:, : 2 * BOX]
            width = values.shape[1]
            along_y, along_x = grid_rows(kx_first + row, width)
            inside = along_y <= own_slope * along_x
            values = jnp.where(inside, values * (1.0 / BOX), 0.0)
            weighted_ref[pl.ds(first, chunk), row * 2 * BOX : row * 2 * BOX + width] = values.astype(
                BF16
            )
        result = lax.dot_general(
            weighted_ref[pl.ds(first, chunk), :],
            rot_ref[...],
            (((1,), (1,)), ((), ())),
            preferred_element_type=F32,
        )
        pad = partial_ref.shape[2] - owned
        result = jnp.concatenate([result, jnp.zeros((chunk, pad), F32)], axis=1)
        for line in range(chunk // share):
            partial_ref[block * (chunk // share) + line] = result[line * share : (line + 1) * share]

    out_copy = pltpu.make_async_copy(weighted_ref, weighted_hbm, l_sem.at[2])
    each(lambda peer: part_copy(peer, me).start())
    out_copy.start()
    scores[me] = partial_ref[me]
    each(lambda peer: part_copy(peer, number(peer)).wait_recv())
    width = scores.shape[2]
    lane = lax.broadcasted_iota(jnp.int32, (share, width), 1)
    real = lane < owned
    halves = []
    for half in range(orients):
        total = jnp.zeros((share, width), F32)
        for block in range(doms):
            for c in range(shells):
                total = total + scores[(block * orients + half) * shells + c]
        halves.append(jnp.where(real, total * (6.0 / BOX), -3e38))
    top = halves[0]
    for half in halves[1:]:
        top = jnp.maximum(top, half)
    row_top = jnp.max(top, axis=1, keepdims=True)
    shifted = [jnp.where(real, jnp.exp(half - row_top), 0.0) for half in halves]
    row_sum = shifted[0]
    for half in shifted[1:]:
        row_sum = row_sum + half
    row_total = jnp.sum(row_sum, axis=1, keepdims=True)
    logz = row_top + jnp.log(row_total)
    for half in range(orients):
        rounded = (shifted[half] / row_total).astype(BF16)
        outgoing[half] = rounded.astype(outgoing.dtype)
    own_slot = orient * shells + shell
    logz_ref[own_slot] = jnp.broadcast_to(logz, logz_ref.shape[1:])
    each(lambda peer: weight_copy(peer, me).start())
    in_dom = near(dom, True)
    for peer in in_dom:
        logz_copy(peer, own_slot).start()
    weights_ref[me] = outgoing[orient]
    out_copy.wait()

    def finish(peer):
        part_copy(peer, me).wait_send()
        weight_copy(peer, me).wait_send()

    each(lambda peer: weight_copy(peer, number(peer)).wait_recv())
    each(finish)
    for peer in in_dom:
        logz_copy(peer, peer[1] * shells + peer[2]).wait_recv()
    for peer in in_dom:
        logz_copy(peer, own_slot).wait_send()


def assign(particle_tile, particle_offset, wedge_slope, tiles, rot_ref, peers):
    doms, orients, shells = peers
    count = doms * orients * shells
    tile_dev, side, _ = tiles.shape
    sub_rows = BOX // (doms * shells)
    rows = round_up(2 * sub_rows, 8)
    shifts = side - BOX + 1
    angle = 2.0 * math.pi / BOX
    kx = np.arange(BOX)
    phase = angle * ((kx[:, None] * kx[None, :]) % BOX)
    x_table = np.zeros((doms * shells, rows, LANES), np.float32)
    for position in range(doms * shells):
        own = slice(position * sub_rows, (position + 1) * sub_rows)
        x_table[position, :sub_rows, :BOX] = np.cos(phase[own])
        x_table[position, sub_rows : 2 * sub_rows, :BOX] = -np.sin(phase[own])
    y_real = np.zeros((2 * LANES, 2 * BOX), np.float32)
    y_real[:BOX, :BOX] = np.cos(phase)
    y_real[:BOX, BOX:] = -np.sin(phase)
    y_real[LANES : LANES + BOX, :BOX] = np.sin(phase)
    y_real[LANES : LANES + BOX, BOX:] = np.cos(phase)
    gap = 2 * LANES - 2 * BOX
    rest = np.stack([np.pad(y_real, ((0, 0), (0, gap))), np.pad(y_real, ((0, 0), (gap, 0)))])
    y_table = []
    for _ in range(3):
        y_table.append(rest.astype(BF16))
        rest = rest - y_table[-1].astype(np.float32)
    y_table = np.stack(y_table, axis=1)
    particles = particle_tile.shape[0]
    owned, depth = rot_ref.shape
    width = round_up(owned, LANES)
    blocks = (count, particles // count, width)
    dma = pltpu.SemaphoreType.DMA
    kind = BF16 if blocks[1] % 16 == 0 else F32
    weighted, weights, logz, hot = pl.pallas_call(
        functools.partial(assign_kernel, peers, sub_rows, owned),
        out_shape=(
            jax.ShapeDtypeStruct((particles, depth), BF16),
            jax.ShapeDtypeStruct(blocks, kind),
            jax.ShapeDtypeStruct((orients * shells, blocks[1], LANES), F32),
            jax.ShapeDtypeStruct((particles, LANES), BF16),
        ),
        in_specs=[SMEM, SMEM, SMEM, VMEM, VMEM, ANY, ANY],
        out_specs=(ANY, VMEM, VMEM, VMEM),
        scratch_shapes=[
            pltpu.VMEM(y_table.shape, BF16),
            pltpu.VMEM(rot_ref.shape, BF16),
            pltpu.VMEM((particles, depth), BF16),
            dma((3,)),
            pltpu.VMEM((doms * tile_dev * side, side), BF16),
            pltpu.VMEM((doms * tile_dev, side, side), BF16),
            pltpu.VMEM((shifts, round_up(3 * rows, 16), LANES), BF16),
            pltpu.VMEM((particles * rows, LANES), F32),
            pltpu.VMEM((particles, LANES), F32),
            pltpu.VMEM((particles, LANES), jnp.int32),
            pltpu.VMEM(blocks, F32),
            pltpu.VMEM(blocks, F32),
            pltpu.VMEM((orients,) + blocks[1:], kind),
            dma((doms,)),
            dma((doms,)),
            dma((doms, orients)),
            dma((doms, orients)),
            dma((doms, orients, shells)),
            dma((doms, orients, shells)),
            dma((count,)),
            dma((count,)),
            dma((count,)),
            dma((count,)),
            dma((orients * shells,)),
            dma((orients * shells,)),
        ],
        compiler_params=pltpu.CompilerParams(
            collective_id=0, has_side_effects=True, vmem_limit_bytes=LIMIT
        ),
        name="assign",
    )(particle_tile, particle_offset.T, wedge_slope, tiles.reshape(tile_dev * side, side), x_table, y_table, rot_ref)
    return weighted, weights.reshape(particles, width), logz.reshape(-1, LANES), hot


def average_kernel(
    sub_rows, shells, owned, slope_ref, weights_ref, rows_ref, weighted_ref, hot_ref, out_ref, logz_ref
):
    dom = lax.axis_index("dom")
    position = dom * shells + lax.axis_index("shell")
    logz_ref[...] = rows_ref[...].T[:1]
    kept = weights_ref[...].astype(F32).T[:owned].astype(BF16)
    tomo_weight = jnp.dot(kept, hot_ref[...], preferred_element_type=F32)[:, :TOMOS]
    pieces = []
    rest = tomo_weight
    for _ in range(3):
        piece = rest.astype(BF16)
        pieces.append(piece.astype(F32))
        rest = rest - pieces[-1]
    pieces = jnp.concatenate(pieces, axis=1).astype(BF16)
    tomo_row = lax.broadcasted_iota(jnp.int32, (TOMOS, 1), 0)
    slopes = jnp.zeros((TOMOS, 1), F32)
    for tomo in range(TOMOS):
        slopes = jnp.where(tomo_row == tomo, slope_ref[tomo].astype(F32), slopes)
    for row in range(0, sub_rows, 2):
        width = min(2, sub_rows - row) * 2 * BOX
        along_y, along_x = grid_rows(position * sub_rows + row, width)
        wedge = jnp.where(along_y <= slopes * along_x, 1.0, 0.0)
        wedge = jnp.concatenate([wedge, wedge, wedge], axis=0).astype(BF16)
        span = slice(row * 2 * BOX, row * 2 * BOX + width)
        numerator = jnp.dot(kept, weighted_ref[:, span], preferred_element_type=F32)
        denominator = jnp.dot(pieces, wedge, preferred_element_type=F32)
        out_ref[:, span] = numerator / (denominator + 1.0)


def average(wedge_slope, weights, rows, weighted, hot, owned, doms, shells):
    part_dev = weights.shape[0] // doms
    return pl.pallas_call(
        functools.partial(average_kernel, BOX // (doms * shells), shells, owned),
        out_shape=(
            jax.ShapeDtypeStruct((owned, weighted.shape[1]), F32),
            jax.ShapeDtypeStruct((1, part_dev), F32),
        ),
        in_specs=[SMEM, VMEM, VMEM, VMEM, VMEM],
        out_specs=(VMEM, VMEM),
        compiler_params=pltpu.CompilerParams(vmem_limit_bytes=LIMIT),
        name="average",
    )(wedge_slope, weights, rows, weighted, hot)


def local(tiles, particle_tile, particle_offset, wedge_slope, rot_ref):
    doms = lax.axis_size("dom")
    orients = lax.axis_size("orient")
    shells = lax.axis_size("shell")
    weighted, weights, rows, hot = assign(
        particle_tile, particle_offset, wedge_slope, tiles, rot_ref, (doms, orients, shells)
    )
    owned = rot_ref.shape[0]
    new_reference, logz = average(wedge_slope, weights, rows, weighted, hot, owned, doms, shells)
    return new_reference, logz.reshape(-1)


def solution(mesh):
    in_specs = (
        P(("groups", "dom"), None, None),
        P("groups"),
        P("groups", None),
        P("groups"),
        P(("groups", "orient"), ("dom", "shell")),
    )
    out_specs = (P(("groups", "orient"), ("dom", "shell")), P(("groups", "dom")))
    return jax.shard_map(local, mesh=mesh, in_specs=in_specs, out_specs=out_specs, check_vma=False)
```
